512 devices in a mesh: ctx: 128 (over x, y, z_hi, core), batch: 4 (over z_lo).
Axes of the slice: x: 4, y: 8, z: 8 (z_hi: 2, z_lo: 4; z = z_hi * 4 + z_lo), core: 2. Of those that a mesh axis runs over, the one named last changes fastest.
Arguments:
- query_rows: bfloat16 [131072, 1024], P(('batch', 'ctx')), parts along dimension 0, may hold values from -6 to 6
- key_rows: bfloat16 [131072, 128], P(('batch', 'ctx')), parts along dimension 0, may hold values from -6 to 6
- value_rows: bfloat16 [131072, 128], P(('batch', 'ctx')), parts along dimension 0, may hold values from -6 to 6
- out_grad: bfloat16 [131072, 1024], P(('batch', 'ctx')), parts along dimension 0, may hold values from -6 to 6
- log_norm: float32 [8, 131072], P(None, ('batch', 'ctx')), parts along dimension 1, may hold values from 3 to 5
- row_dot: float32 [8, 131072], P(None, ('batch', 'ctx')), parts along dimension 1, may hold values from -24 to 24
- span_order: int32 [512], P('batch'), parts along dimension 0, may hold values from 0 to 127, each once
Outputs:
- query_grad: bfloat16 [131072, 1024], P(('batch', 'ctx')), parts along dimension 0
- key_grad: bfloat16 [131072, 128], P(('batch', 'ctx')), parts along dimension 0
- value_grad: bfloat16 [131072, 128], P(('batch', 'ctx')), parts along dimension 0
The draws below stay inside these ranges and needn't reach their ends.
There are 4 independent parts, one for each index of `batch`. The reference program is written for one: setup_inputs(seed, part) draws one part's arguments, and reference() takes and returns one part's arrays. A program takes and returns all parts, laid end to end along the dimension named above; each array names one. Nothing has to cross between parts.
Inputs may be any that keep to these rules, and one draw needn't show every extreme that they name: span_order holds every number from 0 to 128 - 1 once.
All inputs are finite; a program needn't handle non-finite values.
Results may differ from the reference program's by a relative error of at most 0.0049.
Values may be sent and summed in bfloat16 or wider, within the bound.
A program may use at most 64 MiB of HBM per device.

```python
import math
import jax
import jax.numpy as jnp
from jax import lax

H = 8
HD = 128
TOK_DEV = 256
TOKENS = 32768
N_CTX = 128


def block_scale(rng, extent, cuts, least, largest):
    gain = 1.0
    for axis_at, shards_of in cuts:
        steps = jax.random.uniform(jax.random.fold_in(jax.random.fold_in(rng, 6), axis_at), (shards_of,), jnp.float32, least / len(cuts), largest / len(cuts))
        gain = gain * jnp.repeat(jnp.exp(steps), extent[axis_at] // shards_of).reshape((-1,) + (1,) * (len(extent) - 1 - axis_at))
    return gain


def normal_values(key, dims, scale, bound, split=(), held_as=jnp.bfloat16):
    gain = block_scale(key, dims, split, -0.22, 0.18) if split else 1.0
    array = jax.random.normal(key, dims, jnp.float32) * scale * gain
    return jnp.minimum(jnp.maximum(array, -bound), bound).astype(held_as)


def setup_inputs(seed: int = 0, part: int = 0) -> dict:
    splits = jax.random.split(jax.random.key(seed), 8)
    own_keys = jax.random.split(jax.random.fold_in(splits[7], part), 8)
    return {
        "query_rows": normal_values(own_keys[0], (TOKENS, H * HD), 1.0, 6.0, ((0, 128),)),
        "key_rows": normal_values(own_keys[1], (TOKENS, HD), 1.0, 6.0, ((0, 128),)),
        "value_rows": normal_values(own_keys[2], (TOKENS, HD), 1.0, 6.0, ((0, 128),)),
        "out_grad": normal_values(own_keys[3], (TOKENS, H * HD), 1.0, 6.0, ((0, 128),)),
        "log_norm": jnp.clip(3.0 + 2.0 * jax.random.uniform(own_keys[4], (H, TOKENS), jnp.float32) ** block_scale(own_keys[4], (H, TOKENS), ((1, 128),), -0.2, 0.2), 3.0, 5.0),
        "row_dot": normal_values(own_keys[5], (H, TOKENS), 4.0, 24.0, ((1, 128),), jnp.float32),
        "span_order": jax.random.permutation(own_keys[6], N_CTX).astype(jnp.int32),
    }


def dot_nt(left, right):
    return lax.dot_general(left, right, (((1,), (1,)), ((), ())), preferred_element_type=jnp.float32)

def dot_tn(left, right):
    return lax.dot_general(left, right, (((0,), (0,)), ((), ())), preferred_element_type=jnp.float32)

def positions(early, rows, count):
    half = rows // 2
    offsets = jnp.arange(half, dtype=jnp.int32)
    first = early * half + offsets
    second = (2 * count - 1 - early) * half + offsets
    return jnp.concatenate([first, second]).astype(jnp.int32)

def pair_grads(query_rows, out_grad, log_norm, row_dot, key_rows, value_rows, allowed):
    heads = log_norm.shape[0]
    width = key_rows.shape[1]
    inv_root = 1.0 / math.sqrt(width)

    def head_step(head, carry):
        query_grad, key_grad, value_grad = carry
        query_head = lax.dynamic_slice_in_dim(query_rows, head * width, width, 1)
        grad_head = lax.dynamic_slice_in_dim(out_grad, head * width, width, 1)
        norm_head = lax.dynamic_index_in_dim(log_norm, head, 0, keepdims=False)
        dot_head = lax.dynamic_index_in_dim(row_dot, head, 0, keepdims=False)
        scores = dot_nt(query_head, key_rows) * inv_root
        weights = jnp.exp(scores - norm_head[:, None])
        weights = jnp.where(allowed, weights, jnp.zeros_like(weights))
        value_grad = value_grad + dot_tn(weights.astype(jnp.bfloat16), grad_head)
        prob_grad = dot_nt(grad_head, value_rows)
        score_grad = (weights * (prob_grad - dot_head[:, None])).astype(jnp.bfloat16)
        head_query = jnp.dot(score_grad, key_rows, preferred_element_type=jnp.float32) * inv_root
        query_grad = lax.dynamic_update_slice_in_dim(query_grad, head_query, head * width, 1)
        key_grad = key_grad + dot_tn(score_grad, query_head) * inv_root
        return (query_grad, key_grad, value_grad)
    start = (jnp.zeros((query_rows.shape[0], heads * width), jnp.float32), jnp.zeros((key_rows.shape[0], width), jnp.float32), jnp.zeros((key_rows.shape[0], width), jnp.float32))
    return lax.fori_loop(0, heads, head_step, start)

def reference(query_rows, key_rows, value_rows, out_grad, log_norm, row_dot, span_order):
    count = N_CTX
    rows = TOK_DEV
    query_dev = query_rows.reshape(count, rows, -1)
    grad_dev = out_grad.reshape(count, rows, -1)
    key_dev = key_rows.reshape(count, rows, -1)
    value_dev = value_rows.reshape(count, rows, -1)
    norm_dev = jnp.transpose(log_norm.reshape(log_norm.shape[0], count, rows), (1, 0, 2))
    dot_dev = jnp.transpose(row_dot.reshape(row_dot.shape[0], count, rows), (1, 0, 2))
    offsets = (0, 1, count // 2)

    def per_device(index):
        own_pos = positions(span_order[index], rows, count)
        total = jnp.zeros((rows, query_dev.shape[2]), jnp.float32)
        key_terms = []
        value_terms = []
        for offset in offsets:
            source = ((index - offset + count) % count).astype(jnp.int32)
            key_pos = positions(span_order[source], rows, count)
            allowed = own_pos[:, None] >= key_pos[None, :]
            query_part, key_part, value_part = pair_grads(query_dev[index], grad_dev[index], norm_dev[index], dot_dev[index], key_dev[source], value_dev[source], allowed)
            total = total + query_part
            key_terms.append(key_part)
            value_terms.append(value_part)
        return (total, jnp.stack(key_terms), jnp.stack(value_terms))
    query_all, key_all, value_all = lax.map(per_device, jnp.arange(count, dtype=jnp.int32))
    key_grad = jnp.zeros((count, rows, key_all.shape[3]), jnp.float32)
    value_grad = jnp.zeros((count, rows, value_all.shape[3]), jnp.float32)
    for slot, offset in enumerate(offsets):
        key_grad = key_grad + jnp.roll(key_all[:, slot], -offset, axis=0)
        value_grad = value_grad + jnp.roll(value_all[:, slot], -offset, axis=0)
    return (query_all.reshape(count * rows, -1).astype(jnp.bfloat16), key_grad.reshape(count * rows, -1).astype(jnp.bfloat16), value_grad.reshape(count * rows, -1).astype(jnp.bfloat16))
```

```python
import functools
import math

import jax
import jax.numpy as jnp
from jax import lax
from jax.experimental import pallas as pl
from jax.experimental.pallas import tpu as pltpu
from jax.sharding import PartitionSpec as P

MESH = pl.DeviceIdType.MESH
BF16, F32 = jnp.bfloat16, jnp.float32
NEAR, FAR = 0, 1
OWN_EE, OWN_LE, OWN_LL, PARTNER = 0, 1, 2, 3


def dot_nt(left, right):
    return lax.dot_general(left, right, (((1,), (1,)), ((), ())), preferred_element_type=F32)


def dot_nn(left, right):
    return jnp.dot(left, right, preferred_element_type=F32)


def kernel(
    n, heads, half, width,
    query_hbm, key_hbm, value_hbm, grad_hbm, norm_hbm, dot_hbm, span_hbm,
    query_out, key_out, value_out,
    query, grad, norm, dot, keys, values, span,
    got, part, back, score_grads, own_key, own_value,
    local_sem, span_sem, send_sem, recv_sem, part_send_sem, back_sem,
):
    me = lax.axis_index("ctx")
    right, left = lax.rem(me + 1, n), lax.rem(me + n - 1, n)
    across = lax.rem(me + n // 2, n)
    inv_root = 1.0 / math.sqrt(width)

    barrier = pltpu.get_barrier_semaphore()
    for device in (right, left, across):
        pl.semaphore_signal(barrier, inc=1, device_id={"ctx": device}, device_id_type=MESH)

    loads = []
    for source, target in ((key_hbm, keys), (value_hbm, values), (query_hbm, query), (grad_hbm, grad)):
        for block in range(2):
            loads.append((source.at[pl.ds(block * half, half)], target.at[block]))
    for source, target in ((norm_hbm, norm), (dot_hbm, dot)):
        for block in range(2):
            loads.append((source.at[:, pl.ds(block * half, half)], target.at[block]))
    loads = [
        pltpu.make_async_copy(source, target, local_sem.at[i])
        for i, (source, target) in enumerate(loads)
    ]
    span_load = pltpu.make_async_copy(span_hbm, span, span_sem)
    for load in loads:
        load.start()
    span_load.start()

    def offer(slot, block, which, device):
        source = (key_hbm, value_hbm)[which].at[pl.ds(block * half, half)]
        return pltpu.make_async_remote_copy(
            src_ref=source,
            dst_ref=got.at[slot, block, which],
            send_sem=send_sem.at[slot, block, which],
            recv_sem=recv_sem.at[slot, block, which],
            device_id={"ctx": device},
            device_id_type=MESH,
        )

    pl.semaphore_wait(barrier, 3)
    offers = {}
    for block in range(2):
        for slot, device in ((NEAR, right), (FAR, across)):
            for which in range(2):
                offers[slot, block, which] = offer(slot, block, which, device)
                offers[slot, block, which].start()

    for load in loads:
        load.wait()
    span_load.wait()
    own_span = span[me]

    causal = lax.broadcasted_iota(jnp.int32, (half, 2 * half), 0) <= (
        lax.broadcasted_iota(jnp.int32, (half, 2 * half), 1) % half
    )

    def block_grads(key_block, value_block, at, slot, diagonal):
        key_term = value_term = None
        for pair in range(heads // 2):
            cols = [pl.ds((2 * pair + i) * width, width) for i in range(2)]
            rows = [pl.ds(2 * pair + i, 1) for i in range(2)]
            query_two = jnp.concatenate([query[at, :, c] for c in cols], axis=0)
            grad_two = jnp.concatenate([grad[at, :, c] for c in cols], axis=0)
            norm_two = jnp.concatenate([norm[at, r, :] for r in rows], axis=1)
            dot_two = jnp.concatenate([dot[at, r, :] for r in rows], axis=1)
            scores = dot_nt(key_block, query_two) * inv_root
            weights = jnp.exp(scores - norm_two)
            if diagonal:
                weights = jnp.where(causal, weights, 0.0)
            prob_grad = dot_nt(value_block, grad_two)
            score_grad = (weights * (prob_grad - dot_two)).astype(BF16)
            score_grads[slot, :, pl.ds(pair * 2 * half, 2 * half)] = score_grad
            value_now = dot_nn(weights.astype(BF16), grad_two)
            key_now = dot_nn(score_grad, query_two)
            value_term = value_now if pair == 0 else value_term + value_now
            key_term = key_now if pair == 0 else key_term + key_now
        return key_term * inv_root, value_term

    key_term, value_term = block_grads(keys[0], values[0], 0, OWN_EE, True)
    key_more, value_more = block_grads(keys[0], values[0], 1, OWN_LE, False)
    own_key[0] = key_term + key_more
    own_value[0] = value_term + value_more
    own_key[1], own_value[1] = block_grads(keys[1], values[1], 1, OWN_LL, True)

    odd = lax.rem(me, 2)

    def partner(step, _):
        slot = lax.rem(step + 1 + odd, 2)
        source = jnp.where(slot == NEAR, left, across)
        other_span = span[source]
        second = jnp.where(other_span < own_span, 0, 1)

        def give(turn, which):
            return pltpu.make_async_remote_copy(
                src_ref=part.at[slot, turn, which],
                dst_ref=back.at[slot, turn, which],
                send_sem=part_send_sem.at[slot, turn, which],
                recv_sem=back_sem.at[slot, turn, which],
                device_id={"ctx": source},
                device_id_type=MESH,
            )

        for turn in range(2):
            for which in range(2):
                pltpu.make_async_copy(
                    got.at[slot, turn, which], got.at[slot, turn, which], recv_sem.at[slot, turn, which]
                ).wait()
            key_block, value_block = got[slot, 0, 0], got[slot, 0, 1]
            if turn == 1:
                key_block = jnp.where(second == 0, key_block, got[slot, 1, 0])
                value_block = jnp.where(second == 0, value_block, got[slot, 1, 1])
            key_term, value_term = block_grads(
                key_block, value_block, second if turn else 1, PARTNER + 2 * slot + turn, False
            )
            part[slot, turn, 0] = key_term.astype(BF16)
            part[slot, turn, 1] = value_term.astype(BF16)
            for which in range(2):
                give(turn, which).start()
        return 0

    lax.fori_loop(0, 2, partner, 0)

    near_early = span[left] < own_span
    far_early = span[across] < own_span

    def second_keys(slot, early):
        return jnp.where(early, got[slot, 0, 0], got[slot, 1, 0])

    zero = jnp.zeros((half, width), BF16)
    near_second, far_second = second_keys(NEAR, near_early), second_keys(FAR, far_early)
    near_slot, far_slot = PARTNER + 2 * NEAR, PARTNER + 2 * FAR
    early_keys = jnp.concatenate(
        [keys[0], jnp.where(near_early, near_second, zero), jnp.where(far_early, far_second, zero)], axis=0
    ).T
    late_keys = jnp.concatenate(
        [
            keys[0], keys[1], got[NEAR, 0, 0], got[FAR, 0, 0],
            jnp.where(near_early, zero, near_second), jnp.where(far_early, zero, far_second),
        ],
        axis=0,
    ).T
    early_slots = (OWN_EE, near_slot + 1, far_slot + 1)
    late_slots = (OWN_LE, OWN_LL, near_slot, far_slot, near_slot + 1, far_slot + 1)
    stores = []
    for pair in range(heads // 2):
        cols = pl.ds(pair * 2 * half, 2 * half)
        for block, (key_side, slots) in enumerate(((early_keys, early_slots), (late_keys, late_slots))):
            scores = jnp.concatenate([score_grads[s, :, cols] for s in slots], axis=0)
            turned = (dot_nn(key_side, scores) * inv_root).astype(BF16)
            for i in range(2):
                query_out[pl.ds(block * half, half), pl.ds((2 * pair + i) * width, width)] = (
                    turned[:, i * half : (i + 1) * half].T
                )

    for slot in (NEAR, FAR):
        for turn in range(2):
            for which in range(2):
                pltpu.make_async_copy(
                    back.at[slot, turn, which], back.at[slot, turn, which], back_sem.at[slot, turn, which]
                ).wait()
    near_first = own_span < span[right]
    far_first = own_span < span[across]
    for which, (own, out) in enumerate(((own_key, key_out), (own_value, value_out))):
        early = own[0] + back[NEAR, 0, which].astype(F32) + back[FAR, 0, which].astype(F32)
        late = own[1]
        for slot, first in ((NEAR, near_first), (FAR, far_first)):
            term = back[slot, 1, which].astype(F32)
            early = early + jnp.where(first, term, 0.0)
            late = late + jnp.where(first, 0.0, term)
        out[pl.ds(0, half)] = early.astype(BF16)
        out[pl.ds(half, half)] = late.astype(BF16)

    for key in offers:
        offers[key].wait_send()
    for slot in (NEAR, FAR):
        for turn in range(2):
            for which in range(2):
                pltpu.make_async_copy(
                    part.at[slot, turn, which], part.at[slot, turn, which], part_send_sem.at[slot, turn, which]
                ).wait()


def place(query_grad, key_grad, value_grad, query_out, key_out, value_out, sem):
    copies = [
        pltpu.make_async_copy(source, target, sem.at[i])
        for i, (source, target) in enumerate(
            ((query_grad, query_out), (key_grad, key_out), (value_grad, value_out))
        )
    ]
    for copy in copies:
        copy.start()
    for copy in copies:
        copy.wait()


def local(query_rows, key_rows, value_rows, out_grad, log_norm, row_dot, span_order):
    n = lax.axis_size("ctx")
    rows, width = key_rows.shape
    heads, half = log_norm.shape[0], rows // 2
    hbm = pl.BlockSpec(memory_space=pltpu.HBM)
    vmem = pl.BlockSpec(memory_space=pltpu.VMEM)
    blocks = 8 * 3 * half * half * heads * 7
    args = (query_rows, key_rows, value_rows, out_grad, log_norm, row_dot, span_order)
    grads = pl.pallas_call(
        functools.partial(kernel, n, heads, half, width),
        name="attention_grads",
        out_shape=(
            pltpu.VMEM(query_rows.shape, BF16),
            pltpu.VMEM(key_rows.shape, BF16),
            pltpu.VMEM(value_rows.shape, BF16),
        ),
        in_specs=[hbm] * 7,
        out_specs=(vmem, vmem, vmem),
        scratch_shapes=[
            pltpu.VMEM((2, half, heads * width), BF16),
            pltpu.VMEM((2, half, heads * width), BF16),
            pltpu.VMEM((2, heads, half), F32),
            pltpu.VMEM((2, heads, half), F32),
            pltpu.VMEM((2, half, width), BF16),
            pltpu.VMEM((2, half, width), BF16),
            pltpu.SMEM((n,), jnp.int32),
            pltpu.VMEM((2, 2, 2, half, width), BF16),
            pltpu.VMEM((2, 2, 2, half, width), BF16),
            pltpu.VMEM((2, 2, 2, half, width), BF16),
            pltpu.VMEM((7, half, heads * half), BF16),
            pltpu.VMEM((2, half, width), F32),
            pltpu.VMEM((2, half, width), F32),
            pltpu.SemaphoreType.DMA((12,)),
            pltpu.SemaphoreType.DMA,
            pltpu.SemaphoreType.DMA((2, 2, 2)),
            pltpu.SemaphoreType.DMA((2, 2, 2)),
            pltpu.SemaphoreType.DMA((2, 2, 2)),
            pltpu.SemaphoreType.DMA((2, 2, 2)),
        ],
        compiler_params=pltpu.CompilerParams(
            collective_id=0, has_side_effects=True, vmem_limit_bytes=24 * 1024 * 1024
        ),
        cost_estimate=pl.CostEstimate(
            flops=10 * half * half * width * heads * 7, bytes_accessed=2 << 20, transcendentals=blocks // 24
        ),
    )(*[pltpu.with_memory_space_constraint(x, pltpu.HBM) for x in args])
    return pl.pallas_call(
        place,
        name="place_grads",
        out_shape=tuple(pltpu.HBM(g.shape, g.dtype) for g in grads),
        in_specs=[vmem] * 3,
        out_specs=(hbm,) * 3,
        scratch_shapes=[pltpu.SemaphoreType.DMA((3,))],
    )(*[pltpu.with_memory_space_constraint(g, pltpu.VMEM) for g in grads])


def solution(mesh):
    return jax.shard_map(
        local,
        mesh=mesh,
        in_specs=(
            P(("batch", "ctx"), None),
            P(("batch", "ctx"), None),
            P(("batch", "ctx"), None),
            P(("batch", "ctx"), None),
            P(None, ("batch", "ctx")),
            P(None, ("batch", "ctx")),
            P("batch"),
        ),
        out_specs=(P(("batch", "ctx"), None), P(("batch", "ctx"), None), P(("batch", "ctx"), None)),
        check_vma=False,
    )
```

```python
import functools
import math

import jax
import jax.numpy as jnp
from jax import lax
from jax.experimental import pallas as pl
from jax.experimental.pallas import tpu as pltpu
from jax.sharding import PartitionSpec as P

MESH = pl.DeviceIdType.MESH
BF16, F32 = jnp.bfloat16, jnp.float32
NEAR, FAR = 0, 1
OWN_EE, OWN_LE, OWN_LL, PARTNER = 0, 1, 2, 3


def dot_nt(left, right):
    return lax.dot_general(left, right, (((1,), (1,)), ((), ())), preferred_element_type=F32)


def dot_nn(left, right):
    return jnp.dot(left, right, preferred_element_type=F32)


def kernel(
    n, heads, half, width,
    query_hbm, key_hbm, value_hbm, grad_hbm, norm_hbm, dot_hbm, span_hbm,
    query_out, key_out, value_out,
    query, grad, norm, dot, keys, values, span,
    got, part, back, score_grads, own_key, own_value,
    near_ready, far_ready, relay, local_sem, span_sem, send_sem, recv_sem, part_send_sem, back_sem,
):
    me = lax.axis_index("ctx")
    right, left = lax.rem(me + 1, n), lax.rem(me + n - 1, n)
    across = lax.rem(me + n // 2, n)
    inv_root = 1.0 / math.sqrt(width)

    kind = lax.rem(me, 4)
    barrier = pltpu.get_barrier_semaphore()

    def tell(sem, device):
        pl.semaphore_signal(sem, inc=1, device_id={"ctx": device}, device_id_type=MESH)

    @pl.when(kind == 0)
    def _():
        tell(barrier, left)
        tell(barrier, across)

    @pl.when(kind == 1)
    def _():
        tell(barrier, right)
        tell(barrier, across)
        tell(barrier, left)

    @pl.when(kind == 2)
    def _():
        tell(barrier, right)
        pl.semaphore_wait(barrier, 1)
        tell(near_ready, left)

    @pl.when(kind == 3)
    def _():
        tell(barrier, across)

    loads = []
    for source, target in ((key_hbm, keys), (value_hbm, values), (query_hbm, query), (grad_hbm, grad)):
        for block in range(2):
            loads.append((source.at[pl.ds(block * half, half)], target.at[block]))
    for source, target in ((norm_hbm, norm), (dot_hbm, dot)):
        for block in range(2):
            loads.append((source.at[:, pl.ds(block * half, half)], target.at[block]))
    loads = [
        pltpu.make_async_copy(source, target, local_sem.at[i])
        for i, (source, target) in enumerate(loads)
    ]
    span_load = pltpu.make_async_copy(span_hbm, span, span_sem)
    for load in loads:
        load.start()
    span_load.start()

    def offer(slot, block, which, device):
        return pltpu.make_async_remote_copy(
            src_ref=(keys, values)[which].at[block],
            dst_ref=got.at[slot, block, which],
            send_sem=send_sem.at[slot, block, which],
            recv_sem=recv_sem.at[slot, block, which],
            device_id={"ctx": device},
            device_id_type=MESH,
        )

    def near_offers():
        for block in range(2):
            for which in range(2):
                offer(NEAR, block, which, right).start()

    def far_offers():
        for block in range(2):
            for which in range(2):
                offer(FAR, block, which, across).start()

    @pl.when(kind != 2)
    def _():
        pl.semaphore_wait(barrier, jnp.where(kind == 0, 2, jnp.where(kind == 3, 3, 1)))

    for load in loads[:4]:
        load.wait()

    @pl.when(kind == 0)
    def _():
        near_offers()
        far_offers()

    @pl.when(kind == 1)
    def _():
        far_offers()

    @pl.when(kind == 2)
    def _():
        pl.semaphore_wait(far_ready, 1)
        near_offers()
        far_offers()

    @pl.when(kind == 3)
    def _():
        tell(relay, across)
        near_offers()
        far_offers()
        pl.semaphore_wait(relay, 1)
        tell(far_ready, left)

    for load in loads[4:]:
        load.wait()
    span_load.wait()
    own_span = span[me]

    causal = lax.broadcasted_iota(jnp.int32, (half, heads * half), 0) <= (
        lax.broadcasted_iota(jnp.int32, (half, heads * half), 1) % half
    )

    def by_head(ref, at):
        return jnp.concatenate([ref[at, :, pl.ds(h * width, width)] for h in range(heads)], axis=0)

    def by_row(ref, at):
        return jnp.concatenate([ref[at, pl.ds(h, 1), :] for h in range(heads)], axis=1)

    def block_grads(key_block, value_block, at, slot, diagonal):
        query_all, grad_all = by_head(query, at), by_head(grad, at)
        weights = jnp.exp(dot_nt(key_block, query_all) * inv_root - by_row(norm, at))
        if diagonal:
            weights = jnp.where(causal, weights, 0.0)
        score_grad = (weights * (dot_nt(value_block, grad_all) - by_row(dot, at))).astype(BF16)
        score_grads[slot] = score_grad
        value_term = dot_nn(weights.astype(BF16), grad_all)
        return dot_nn(score_grad, query_all) * inv_root, value_term

    key_term, value_term = block_grads(keys[0], values[0], 0, OWN_EE, True)
    key_more, value_more = block_grads(keys[0], values[0], 1, OWN_LE, False)
    own_key[0] = key_term + key_more
    own_value[0] = value_term + value_more
    own_key[1], own_value[1] = block_grads(keys[1], values[1], 1, OWN_LL, True)

    far_first = jnp.where(kind == 0, 1, 0)

    def partner(step, _):
        slot = lax.rem(step + far_first, 2)

        @pl.when((kind == 1) & (step == 1))
        def _():
            pl.semaphore_wait(near_ready, 1)
            near_offers()

        source = jnp.where(slot == NEAR, left, across)
        other_span = span[source]
        second = jnp.where(other_span < own_span, 0, 1)

        def give(turn, which):
            return pltpu.make_async_remote_copy(
                src_ref=part.at[slot, turn, which],
                dst_ref=back.at[slot, turn, which],
                send_sem=part_send_sem.at[slot, turn, which],
                recv_sem=back_sem.at[slot, turn, which],
                device_id={"ctx": source},
                device_id_type=MESH,
            )

        for turn in range(2):
            for which in range(2):
                pltpu.make_async_copy(
                    got.at[slot, turn, which], got.at[slot, turn, which], recv_sem.at[slot, turn, which]
                ).wait()
            key_block, value_block = got[slot, 0, 0], got[slot, 0, 1]
            if turn == 1:
                key_block = jnp.where(second == 0, key_block, got[slot, 1, 0])
                value_block = jnp.where(second == 0, value_block, got[slot, 1, 1])
            key_term, value_term = block_grads(
                key_block, value_block, second if turn else 1, PARTNER + 2 * slot + turn, False
            )
            part[slot, turn, 0] = key_term.astype(BF16)
            part[slot, turn, 1] = value_term.astype(BF16)
            for which in range(2):
                give(turn, which).start()
        return 0

    lax.fori_loop(0, 2, partner, 0)

    near_early = span[left] < own_span
    far_early = span[across] < own_span

    def second_keys(slot, early):
        return jnp.where(early, got[slot, 0, 0], got[slot, 1, 0])

    zero = jnp.zeros((half, width), BF16)
    near_second, far_second = second_keys(NEAR, near_early), second_keys(FAR, far_early)
    near_slot, far_slot = PARTNER + 2 * NEAR, PARTNER + 2 * FAR
    early_keys = jnp.concatenate(
        [keys[0], jnp.where(near_early, near_second, zero), jnp.where(far_early, far_second, zero)], axis=0
    ).T
    late_keys = jnp.concatenate(
        [
            keys[0], keys[1], got[NEAR, 0, 0], got[FAR, 0, 0],
            jnp.where(near_early, zero, near_second), jnp.where(far_early, zero, far_second),
        ],
        axis=0,
    ).T
    early_slots = (OWN_EE, near_slot + 1, far_slot + 1)
    late_slots = (OWN_LE, OWN_LL, near_slot, far_slot, near_slot + 1, far_slot + 1)
    stores = []
    for pair in range(heads // 2):
        cols = pl.ds(pair * 2 * half, 2 * half)
        for block, (key_side, slots) in enumerate(((early_keys, early_slots), (late_keys, late_slots))):
            scores = jnp.concatenate([score_grads[s, :, cols] for s in slots], axis=0)
            turned = (dot_nn(key_side, scores) * inv_root).astype(BF16)
            for i in range(2):
                query_out[pl.ds(block * half, half), pl.ds((2 * pair + i) * width, width)] = (
                    turned[:, i * half : (i + 1) * half].T
                )

    for slot in (NEAR, FAR):
        for turn in range(2):
            for which in range(2):
                pltpu.make_async_copy(
                    back.at[slot, turn, which], back.at[slot, turn, which], back_sem.at[slot, turn, which]
                ).wait()
    near_early_back = own_span < span[right]
    far_early_back = own_span < span[across]
    for which, (own, out) in enumerate(((own_key, key_out), (own_value, value_out))):
        early = own[0] + back[NEAR, 0, which].astype(F32) + back[FAR, 0, which].astype(F32)
        late = own[1]
        for slot, to_early in ((NEAR, near_early_back), (FAR, far_early_back)):
            term = back[slot, 1, which].astype(F32)
            early = early + jnp.where(to_early, term, 0.0)
            late = late + jnp.where(to_early, 0.0, term)
        out[pl.ds(0, half)] = early.astype(BF16)
        out[pl.ds(half, half)] = late.astype(BF16)

    for slot in (NEAR, FAR):
        for turn in range(2):
            for which in range(2):
                offer(slot, turn, which, right if slot == NEAR else across).wait_send()
                pltpu.make_async_copy(
                    part.at[slot, turn, which], part.at[slot, turn, which], part_send_sem.at[slot, turn, which]
                ).wait()


def place(query_grad, key_grad, value_grad, query_out, key_out, value_out, sem):
    copies = [
        pltpu.make_async_copy(source, target, sem.at[i])
        for i, (source, target) in enumerate(
            ((query_grad, query_out), (key_grad, key_out), (value_grad, value_out))
        )
    ]
    for copy in copies:
        copy.start()
    for copy in copies:
        copy.wait()


def local(query_rows, key_rows, value_rows, out_grad, log_norm, row_dot, span_order):
    n = lax.axis_size("ctx")
    rows, width = key_rows.shape
    heads, half = log_norm.shape[0], rows // 2
    hbm = pl.BlockSpec(memory_space=pltpu.HBM)
    vmem = pl.BlockSpec(memory_space=pltpu.VMEM)
    blocks = 8 * 3 * half * half * heads * 7
    args = (query_rows, key_rows, value_rows, out_grad, log_norm, row_dot, span_order)
    grads = pl.pallas_call(
        functools.partial(kernel, n, heads, half, width),
        name="attention_grads",
        out_shape=(
            pltpu.VMEM(query_rows.shape, BF16),
            pltpu.VMEM(key_rows.shape, BF16),
            pltpu.VMEM(value_rows.shape, BF16),
        ),
        in_specs=[hbm] * 7,
        out_specs=(vmem, vmem, vmem),
        scratch_shapes=[
            pltpu.VMEM((2, half, heads * width), BF16),
            pltpu.VMEM((2, half, heads * width), BF16),
            pltpu.VMEM((2, heads, half), F32),
            pltpu.VMEM((2, heads, half), F32),
            pltpu.VMEM((2, half, width), BF16),
            pltpu.VMEM((2, half, width), BF16),
            pltpu.SMEM((n,), jnp.int32),
            pltpu.VMEM((2, 2, 2, half, width), BF16),
            pltpu.VMEM((2, 2, 2, half, width), BF16),
            pltpu.VMEM((2, 2, 2, half, width), BF16),
            pltpu.VMEM((7, half, heads * half), BF16),
            pltpu.VMEM((2, half, width), F32),
            pltpu.VMEM((2, half, width), F32),
            pltpu.SemaphoreType.REGULAR,
            pltpu.SemaphoreType.REGULAR,
            pltpu.SemaphoreType.REGULAR,
            pltpu.SemaphoreType.DMA((12,)),
            pltpu.SemaphoreType.DMA,
            pltpu.SemaphoreType.DMA((2, 2, 2)),
            pltpu.SemaphoreType.DMA((2, 2, 2)),
            pltpu.SemaphoreType.DMA((2, 2, 2)),
            pltpu.SemaphoreType.DMA((2, 2, 2)),
        ],
        compiler_params=pltpu.CompilerParams(
            collective_id=0, has_side_effects=True, vmem_limit_bytes=24 * 1024 * 1024
        ),
        cost_estimate=pl.CostEstimate(
            flops=10 * half * half * width * heads * 7, bytes_accessed=2 << 20, transcendentals=blocks // 24
        ),
    )(*[pltpu.with_memory_space_constraint(x, pltpu.HBM) for x in args])
    return pl.pallas_call(
        place,
        name="place_grads",
        out_shape=tuple(pltpu.HBM(g.shape, g.dtype) for g in grads),
        in_specs=[vmem] * 3,
        out_specs=(hbm,) * 3,
        scratch_shapes=[pltpu.SemaphoreType.DMA((3,))],
    )(*[pltpu.with_memory_space_constraint(g, pltpu.VMEM) for g in grads])


def solution(mesh):
    return jax.shard_map(
        local,
        mesh=mesh,
        in_specs=(
            P(("batch", "ctx"), None),
            P(("batch", "ctx"), None),
            P(("batch", "ctx"), None),
            P(("batch", "ctx"), None),
            P(None, ("batch", "ctx")),
            P(None, ("batch", "ctx")),
            P("batch"),
        ),
        out_specs=(P(("batch", "ctx"), None), P(("batch", "ctx"), None), P(("batch", "ctx"), None)),
        check_vma=False,
    )
```

```python
import functools
import math

import jax
import jax.numpy as jnp
from jax import lax
from jax.experimental import pallas as pl
from jax.experimental.pallas import tpu as pltpu
from jax.sharding import PartitionSpec as P

MESH = pl.DeviceIdType.MESH
BF16, F32 = jnp.bfloat16, jnp.float32
NEAR, FAR = 0, 1
OWN_EE, OWN_LE, OWN_LL, PARTNER = 0, 1, 2, 3


def dot_nt(left, right):
    return lax.dot_general(left, right, (((1,), (1,)), ((), ())), preferred_element_type=F32)


def dot_nn(left, right):
    return jnp.dot(left, right, preferred_element_type=F32)


def kernel(
    n, heads, half, width,
    query_hbm, key_hbm, value_hbm, grad_hbm, norm_hbm, dot_hbm, span_hbm,
    query_out, key_out, value_out,
    query, grad, norm, dot, own, span,
    got, held, part, back, score_grads, own_key, own_value,
    near_ready, far_ready, relay, local_sem, span_sem, send_sem, recv_sem, held_sem, pass_sem, part_send_sem, back_sem,
):
    me = lax.axis_index("ctx")
    right, left = lax.rem(me + 1, n), lax.rem(me + n - 1, n)
    across = lax.rem(me + n // 2, n)
    inv_root = 1.0 / math.sqrt(width)

    kind = lax.rem(me, 4)
    lane, lanes = lax.axis_index("batch"), lax.axis_size("batch")
    low = lane < lanes // 2
    via = jnp.where(low, lane + lanes // 2, lanes - 1 - lane)
    giver = jnp.where(low, lanes - 1 - lane, lane - lanes // 2)
    barrier = pltpu.get_barrier_semaphore()

    def tell(sem, device, at=lane):
        pl.semaphore_signal(sem, inc=1, device_id={"ctx": device, "batch": at}, device_id_type=MESH)

    @pl.when(kind == 0)
    def _():
        tell(barrier, left)
        tell(barrier, across)

    @pl.when(kind == 1)
    def _():
        tell(barrier, lax.rem(me + 2, n), giver)
        tell(barrier, me, giver)
        tell(barrier, across)
        tell(barrier, left)

    @pl.when(kind == 2)
    def _():
        tell(barrier, right)
        tell(barrier, across)

    @pl.when(kind == 3)
    def _():
        tell(barrier, left)

    quarter = half // 2
    loads = []
    for which, source in enumerate((key_hbm, value_hbm)):
        loads.append((source, own.at[:, which]))
    for source, target in ((query_hbm, query), (grad_hbm, grad)):
        for block in range(2):
            loads.append((source.at[pl.ds(block * half, half)], target.at[block]))
    for source, target in ((norm_hbm, norm), (dot_hbm, dot)):
        for block in range(2):
            loads.append((source.at[:, pl.ds(block * half, half)], target.at[block]))
    loads = [
        pltpu.make_async_copy(source, target, local_sem.at[i])
        for i, (source, target) in enumerate(loads)
    ]
    span_load = pltpu.make_async_copy(span_hbm, span, span_sem)
    for load in loads[:2]:
        load.start()

    @pl.when(kind == 3)
    def _():
        pl.semaphore_wait(barrier, 3)
        tell(near_ready, lax.rem(me + n - 2, n), via)

    for load in loads[2:]:
        load.start()
    span_load.start()

    def offer(slot, piece, device):
        return pltpu.make_async_remote_copy(
            src_ref=own.at[piece],
            dst_ref=got.at[slot, piece],
            send_sem=send_sem.at[slot, piece],
            recv_sem=recv_sem.at[slot, piece],
            device_id={"ctx": device},
            device_id_type=MESH,
        )

    def hand(piece):
        return pltpu.make_async_remote_copy(
            src_ref=own.at[piece],
            dst_ref=held.at[piece],
            send_sem=send_sem.at[NEAR, piece],
            recv_sem=held_sem.at[piece],
            device_id={"ctx": me, "batch": via},
            device_id_type=MESH,
        )

    def pass_on(piece):
        return pltpu.make_async_remote_copy(
            src_ref=held.at[piece],
            dst_ref=got.at[NEAR, piece],
            send_sem=pass_sem.at[piece],
            recv_sem=recv_sem.at[NEAR, piece],
            device_id={"ctx": right, "batch": giver},
            device_id_type=MESH,
        )

    def near_offers():
        for piece in range(4):
            offer(NEAR, piece, right).start()

    def far_offers():
        for piece in range(4):
            offer(FAR, piece, across).start()

    @pl.when(kind != 3)
    def _():
        pl.semaphore_wait(barrier, 2)

    for load in loads[:2]:
        load.wait()

    @pl.when(kind == 1)
    def _():
        for piece in range(4):
            hand(piece).start()

    @pl.when(kind != 1)
    def _():
        near_offers()

    @pl.when(kind == 3)
    def _():
        pl.semaphore_wait(far_ready, 1)

    far_offers()

    @pl.when(kind == 2)
    def _():
        tell(relay, across)
        pl.semaphore_wait(relay, 1)
        tell(far_ready, right)

    for load in loads[2:]:
        load.wait()
    span_load.wait()
    own_span = span[me]

    causal = lax.broadcasted_iota(jnp.int32, (half, heads * half), 0) <= (
        lax.broadcasted_iota(jnp.int32, (half, heads * half), 1) % half
    )

    def by_head(ref, at):
        return jnp.concatenate([ref[at, :, pl.ds(h * width, width)] for h in range(heads)], axis=0)

    def by_row(ref, at):
        return jnp.concatenate([ref[at, pl.ds(h, 1), :] for h in range(heads)], axis=1)

    def block_grads(key_block, value_block, at, score_out, diagonal=False):
        query_all, grad_all = by_head(query, at), by_head(grad, at)
        weights = jnp.exp(dot_nt(key_block, query_all) * inv_root - by_row(norm, at))
        if diagonal:
            weights = jnp.where(causal, weights, 0.0)
        score_grad = (weights * (dot_nt(value_block, grad_all) - by_row(dot, at))).astype(BF16)
        score_out[...] = score_grad
        value_term = dot_nn(weights.astype(BF16), grad_all)
        return dot_nn(score_grad, query_all) * inv_root, value_term

    def joined(*pieces):
        return jnp.concatenate(pieces, axis=0)

    own_keys = [joined(own[2 * block, 0], own[2 * block + 1, 0]) for block in range(2)]
    own_values = [joined(own[2 * block, 1], own[2 * block + 1, 1]) for block in range(2)]
    key_term, value_term = block_grads(own_keys[0], own_values[0], 0, score_grads.at[OWN_EE], True)
    key_more, value_more = block_grads(own_keys[0], own_values[0], 1, score_grads.at[OWN_LE])
    own_key[0] = key_term + key_more
    own_value[0] = value_term + value_more
    own_key[1], own_value[1] = block_grads(own_keys[1], own_values[1], 1, score_grads.at[OWN_LL], True)

    far_first = jnp.where(kind == 0, 1, 0)

    def partner(step, _):
        slot = lax.rem(step + far_first, 2)

        @pl.when((kind == 1) & (step == 1))
        def _():
            pl.semaphore_wait(near_ready, 1)
            for piece in range(4):
                hand(piece).wait_recv()
                pass_on(piece).start()

        source = jnp.where(slot == NEAR, left, across)
        other_span = span[source]
        second = jnp.where(other_span < own_span, 0, 1)

        def give(first, count):
            pieces = pl.ds(first, count)
            return pltpu.make_async_remote_copy(
                src_ref=part.at[slot, pieces],
                dst_ref=back.at[slot, pieces],
                send_sem=part_send_sem.at[slot, first],
                recv_sem=back_sem.at[slot, first],
                device_id={"ctx": source},
                device_id_type=MESH,
            )

        def arrive(piece):
            pltpu.make_async_copy(got.at[slot, piece], got.at[slot, piece], recv_sem.at[slot, piece]).wait()

        arrive(0)
        arrive(1)
        score_slot = PARTNER + 2 * slot
        key_term, value_term = block_grads(
            joined(got[slot, 0, 0], got[slot, 1, 0]),
            joined(got[slot, 0, 1], got[slot, 1, 1]),
            1,
            score_grads.at[score_slot],
        )
        for piece in range(2):
            rows = slice(piece * quarter, (piece + 1) * quarter)
            part[slot, piece, 0] = key_term[rows].astype(BF16)
            part[slot, piece, 1] = value_term[rows].astype(BF16)
        give(0, 2).start()

        for piece in range(2):
            arrive(2 + piece)
            key_block, value_block = (
                jnp.where(second == 0, got[slot, piece, which], got[slot, 2 + piece, which]) for which in range(2)
            )
            key_term, value_term = block_grads(
                key_block, value_block, second, score_grads.at[score_slot + 1, pl.ds(piece * quarter, quarter)]
            )
            part[slot, 2 + piece, 0] = key_term.astype(BF16)
            part[slot, 2 + piece, 1] = value_term.astype(BF16)
            give(2 + piece, 1).start()
        return 0

    lax.fori_loop(0, 2, partner, 0)

    near_early = span[left] < own_span
    far_early = span[across] < own_span

    def first_keys(slot):
        return joined(got[slot, 0, 0], got[slot, 1, 0])

    def second_keys(slot, early):
        return jnp.where(early, first_keys(slot), joined(got[slot, 2, 0], got[slot, 3, 0]))

    zero = jnp.zeros((half, width), BF16)
    near_second, far_second = second_keys(NEAR, near_early), second_keys(FAR, far_early)
    near_slot, far_slot = PARTNER + 2 * NEAR, PARTNER + 2 * FAR
    early_keys = joined(
        own_keys[0], jnp.where(near_early, near_second, zero), jnp.where(far_early, far_second, zero)
    ).T
    late_keys = joined(
        own_keys[0], own_keys[1], first_keys(NEAR), first_keys(FAR),
        jnp.where(near_early, zero, near_second), jnp.where(far_early, zero, far_second),
    ).T
    early_slots = (OWN_EE, near_slot + 1, far_slot + 1)
    late_slots = (OWN_LE, OWN_LL, near_slot, far_slot, near_slot + 1, far_slot + 1)
    stores = []
    for pair in range(heads // 2):
        cols = pl.ds(pair * 2 * half, 2 * half)
        for block, (key_side, slots) in enumerate(((early_keys, early_slots), (late_keys, late_slots))):
            scores = jnp.concatenate([score_grads[s, :, cols] for s in slots], axis=0)
            turned = (dot_nn(key_side, scores) * inv_root).astype(BF16)
            for i in range(2):
                query_out[pl.ds(block * half, half), pl.ds((2 * pair + i) * width, width)] = (
                    turned[:, i * half : (i + 1) * half].T
                )

    pieces_back = ((0, 2), (2, 1), (3, 1))
    for slot in (NEAR, FAR):
        for first, count in pieces_back:
            arrived = back.at[slot, pl.ds(first, count)]
            pltpu.make_async_copy(arrived, arrived, back_sem.at[slot, first]).wait()
    near_early_back = own_span < span[right]
    far_early_back = own_span < span[across]
    for which, (sums, out) in enumerate(((own_key, key_out), (own_value, value_out))):
        early, late = sums[0], sums[1]
        for slot, to_early in ((NEAR, near_early_back), (FAR, far_early_back)):
            term = joined(back[slot, 2, which], back[slot, 3, which]).astype(F32)
            early = early + joined(back[slot, 0, which], back[slot, 1, which]).astype(F32)
            early = early + jnp.where(to_early, term, 0.0)
            late = late + jnp.where(to_early, 0.0, term)
        out[pl.ds(0, half)] = early.astype(BF16)
        out[pl.ds(half, half)] = late.astype(BF16)

    for slot in (NEAR, FAR):
        for piece in range(4):
            offer(slot, piece, right if slot == NEAR else across).wait_send()
        for first, count in pieces_back:
            sent = part.at[slot, pl.ds(first, count)]
            pltpu.make_async_copy(sent, sent, part_send_sem.at[slot, first]).wait()

    @pl.when(kind == 1)
    def _():
        for piece in range(4):
            pass_on(piece).wait_send()


def place(query_grad, key_grad, value_grad, query_out, key_out, value_out, sem):
    copies = [
        pltpu.make_async_copy(source, target, sem.at[i])
        for i, (source, target) in enumerate(
            ((query_grad, query_out), (key_grad, key_out), (value_grad, value_out))
        )
    ]
    for copy in copies:
        copy.start()
    for copy in copies:
        copy.wait()


def local(query_rows, key_rows, value_rows, out_grad, log_norm, row_dot, span_order):
    n = lax.axis_size("ctx")
    rows, width = key_rows.shape
    heads, half = log_norm.shape[0], rows // 2
    hbm = pl.BlockSpec(memory_space=pltpu.HBM)
    vmem = pl.BlockSpec(memory_space=pltpu.VMEM)
    blocks = 8 * 3 * half * half * heads * 7
    key_pieces, value_pieces = (x.reshape(4, half // 2, width) for x in (key_rows, value_rows))
    args = (query_rows, key_pieces, value_pieces, out_grad, log_norm, row_dot, span_order)
    grads = pl.pallas_call(
        functools.partial(kernel, n, heads, half, width),
        name="attention_grads",
        out_shape=(
            pltpu.VMEM(query_rows.shape, BF16),
            pltpu.VMEM(key_rows.shape, BF16),
            pltpu.VMEM(value_rows.shape, BF16),
        ),
        in_specs=[hbm] * 7,
        out_specs=(vmem, vmem, vmem),
        scratch_shapes=[
            pltpu.VMEM((2, half, heads * width), BF16),
            pltpu.VMEM((2, half, heads * width), BF16),
            pltpu.VMEM((2, heads, half), F32),
            pltpu.VMEM((2, heads, half), F32),
            pltpu.VMEM((4, 2, half // 2, width), BF16),
            pltpu.SMEM((n,), jnp.int32),
            pltpu.VMEM((2, 4, 2, half // 2, width), BF16),
            pltpu.VMEM((4, 2, half // 2, width), BF16),
            pltpu.VMEM((2, 4, 2, half // 2, width), BF16),
            pltpu.VMEM((2, 4, 2, half // 2, width), BF16),
            pltpu.VMEM((7, half, heads * half), BF16),
            pltpu.VMEM((2, half, width), F32),
            pltpu.VMEM((2, half, width), F32),
            pltpu.SemaphoreType.REGULAR,
            pltpu.SemaphoreType.REGULAR,
            pltpu.SemaphoreType.REGULAR,
            pltpu.SemaphoreType.DMA((10,)),
            pltpu.SemaphoreType.DMA,
            pltpu.SemaphoreType.DMA((2, 4)),
            pltpu.SemaphoreType.DMA((2, 4)),
            pltpu.SemaphoreType.DMA((4,)),
            pltpu.SemaphoreType.DMA((4,)),
            pltpu.SemaphoreType.DMA((2, 4)),
            pltpu.SemaphoreType.DMA((2, 4)),
        ],
        compiler_params=pltpu.CompilerParams(
            collective_id=0, has_side_effects=True, vmem_limit_bytes=24 * 1024 * 1024
        ),
        cost_estimate=pl.CostEstimate(
            flops=10 * half * half * width * heads * 7, bytes_accessed=2 << 20, transcendentals=blocks // 24
        ),
    )(*[pltpu.with_memory_space_constraint(x, pltpu.HBM) for x in args])
    return pl.pallas_call(
        place,
        name="place_grads",
        out_shape=tuple(pltpu.HBM(g.shape, g.dtype) for g in grads),
        in_specs=[vmem] * 3,
        out_specs=(hbm,) * 3,
        scratch_shapes=[pltpu.SemaphoreType.DMA((3,))],
    )(*[pltpu.with_memory_space_constraint(g, pltpu.VMEM) for g in grads])


def solution(mesh):
    return jax.shard_map(
        local,
        mesh=mesh,
        in_specs=(
            P(("batch", "ctx"), None),
            P(("batch", "ctx"), None),
            P(("batch", "ctx"), None),
            P(("batch", "ctx"), None),
            P(None, ("batch", "ctx")),
            P(None, ("batch", "ctx")),
            P("batch"),
        ),
        out_specs=(P(("batch", "ctx"), None), P(("batch", "ctx"), None), P(("batch", "ctx"), None)),
        check_vma=False,
    )
```

```python
import functools
import math

import jax
import jax.numpy as jnp
from jax import lax
from jax.experimental import pallas as pl
from jax.experimental.pallas import tpu as pltpu
from jax.sharding import PartitionSpec as P

MESH = pl.DeviceIdType.MESH
BF16, F32 = jnp.bfloat16, jnp.float32
NEAR, FAR = 0, 1
OWN_EE, OWN_LE, OWN_LL, PARTNER = 0, 1, 2, 3
CHUNKS = 8
PIECES = ((0, 4), (4, 3), (7, 1))


def dot_nt(left, right):
    return lax.dot_general(left, right, (((1,), (1,)), ((), ())), preferred_element_type=F32)


def dot_nn(left, right):
    return jnp.dot(left, right, preferred_element_type=F32)


def kernel(
    n, heads, half, width,
    query_hbm, key_hbm, value_hbm, grad_hbm, norm_hbm, dot_hbm, span_hbm,
    query_out, key_out, value_out,
    sides, rows, own, span,
    got, held, part, back, score_grads, own_key, own_value,
    ready, load_sem, span_sem, send_sem, recv_sem, held_sem, pass_sem, part_send_sem, back_sem,
):
    me = lax.axis_index("ctx")
    right, left = lax.rem(me + 1, n), lax.rem(me + n - 1, n)
    across = lax.rem(me + n // 2, n)
    inv_root = 1.0 / math.sqrt(width)

    kind = lax.rem(me, 4)
    lane, lanes = lax.axis_index("batch"), lax.axis_size("batch")
    low = lane < lanes // 2
    via = jnp.where(low, lane + lanes // 2, lanes - 1 - lane)
    giver = jnp.where(low, lanes - 1 - lane, lane - lanes // 2)
    barrier = pltpu.get_barrier_semaphore()

    def tell(sem, device, at=lane):
        pl.semaphore_signal(sem, inc=1, device_id={"ctx": device, "batch": at}, device_id_type=MESH)

    @pl.when(kind == 0)
    def _():
        tell(barrier, left)
        tell(barrier, across)

    @pl.when(kind == 1)
    def _():
        tell(barrier, lax.rem(me + 2, n), giver)
        tell(barrier, me, giver)
        tell(barrier, across)
        tell(barrier, left)

    @pl.when(kind == 2)
    def _():
        tell(barrier, right)
        tell(barrier, across)

    @pl.when(kind == 3)
    def _():
        tell(barrier, left)

    chunk = 2 * half // CHUNKS
    query, grad, norm, dot = sides.at[0], sides.at[1], rows.at[0], rows.at[1]

    def load(source, target, group):
        pltpu.make_async_copy(source, target, load_sem.at[group]).start()

    def wait_all(ref, sem):
        pltpu.make_async_copy(ref, ref, sem).wait()

    for which, source in enumerate((key_hbm, value_hbm)):
        load(source, own.at[:, which], 0)

    def near_from_hbm():
        for piece, (first, count) in enumerate(PIECES):
            for which, source in enumerate((key_hbm, value_hbm)):
                pltpu.make_async_remote_copy(
                    src_ref=source.at[pl.ds(first, count)],
                    dst_ref=got.at[NEAR, pl.ds(first, count), which],
                    send_sem=send_sem,
                    recv_sem=recv_sem.at[NEAR, piece],
                    device_id={"ctx": right},
                    device_id_type=MESH,
                ).start()

    @pl.when(kind == 3)
    def _():
        pl.semaphore_wait(barrier, 3)
        tell(ready, lax.rem(me + n - 2, n), via)
        near_from_hbm()

    for which, source in enumerate((query_hbm, grad_hbm)):
        for block in range(2):
            load(source.at[pl.ds(block * half, half)], sides.at[which, block], 1)
    for which, source in enumerate((norm_hbm, dot_hbm)):
        for block in range(2):
            load(source.at[:, pl.ds(block * half, half)], rows.at[which, block], 2)
    span_load = pltpu.make_async_copy(span_hbm, span, span_sem)
    span_load.start()

    def offer(slot, piece, device):
        return pltpu.make_async_remote_copy(
            src_ref=own.at[pl.ds(*PIECES[piece])],
            dst_ref=got.at[slot, pl.ds(*PIECES[piece])],
            send_sem=send_sem,
            recv_sem=recv_sem.at[slot, piece],
            device_id={"ctx": device},
            device_id_type=MESH,
        )

    def hand():
        return pltpu.make_async_remote_copy(
            src_ref=own,
            dst_ref=held,
            send_sem=send_sem,
            recv_sem=held_sem,
            device_id={"ctx": me, "batch": via},
            device_id_type=MESH,
        )

    def pass_on(piece):
        return pltpu.make_async_remote_copy(
            src_ref=held.at[pl.ds(*PIECES[piece])],
            dst_ref=got.at[NEAR, pl.ds(*PIECES[piece])],
            send_sem=pass_sem,
            recv_sem=recv_sem.at[NEAR, piece],
            device_id={"ctx": right, "batch": giver},
            device_id_type=MESH,
        )

    def near_offers():
        for piece in range(len(PIECES)):
            offer(NEAR, piece, right).start()

    def far_offers():
        for piece in range(len(PIECES)):
            offer(FAR, piece, across).start()

    @pl.when(kind != 3)
    def _():
        pl.semaphore_wait(barrier, 2)

    wait_all(own, load_sem.at[0])

    @pl.when(kind == 1)
    def _():
        hand().start()

    @pl.when((kind == 0) | (kind == 2))
    def _():
        near_offers()

    @pl.when(kind == 3)
    def _():
        pl.semaphore_wait(ready, 1)

    far_offers()

    @pl.when(kind == 2)
    def _():
        tell(ready, across)
        pl.semaphore_wait(ready, 1)
        tell(ready, right)

    wait_all(sides, load_sem.at[1])
    wait_all(rows, load_sem.at[2])
    span_load.wait()
    own_span = span[me]

    causal = lax.broadcasted_iota(jnp.int32, (half, heads * half), 0) <= (
        lax.broadcasted_iota(jnp.int32, (half, heads * half), 1) % half
    )

    def by_head(ref, at):
        return jnp.concatenate([ref[at, :, pl.ds(h * width, width)] for h in range(heads)], axis=0)

    def by_row(ref, at):
        return jnp.concatenate([ref[at, pl.ds(h, 1), :] for h in range(heads)], axis=1)

    def block_grads(key_block, value_block, at, score_out, diagonal=False):
        query_all, grad_all = by_head(query, at), by_head(grad, at)
        weights = jnp.exp(dot_nt(key_block, query_all) * inv_root - by_row(norm, at))
        if diagonal:
            weights = jnp.where(causal, weights, 0.0)
        score_grad = (weights * (dot_nt(value_block, grad_all) - by_row(dot, at))).astype(BF16)
        score_out[...] = score_grad
        value_term = dot_nn(weights.astype(BF16), grad_all)
        return dot_nn(score_grad, query_all) * inv_root, value_term

    def joined(*pieces):
        return jnp.concatenate(pieces, axis=0)

    def block_of(ref, block, which, slot=()):
        chunks = range(block * CHUNKS // 2, (block + 1) * CHUNKS // 2)
        return joined(*(ref[(*slot, c, which)] for c in chunks))

    own_keys = [block_of(own, block, 0) for block in range(2)]
    own_values = [block_of(own, block, 1) for block in range(2)]
    key_term, value_term = block_grads(own_keys[0], own_values[0], 0, score_grads.at[OWN_EE], True)
    key_more, value_more = block_grads(own_keys[0], own_values[0], 1, score_grads.at[OWN_LE])
    own_key[0] = key_term + key_more
    own_value[0] = value_term + value_more
    own_key[1], own_value[1] = block_grads(own_keys[1], own_values[1], 1, score_grads.at[OWN_LL], True)

    far_first = jnp.where(kind == 0, 1, 0)

    def partner(step, _):
        slot = lax.rem(step + far_first, 2)

        @pl.when((kind == 1) & (step == 1))
        def _():
            pl.semaphore_wait(ready, 1)
            hand().wait_recv()
            for piece in range(len(PIECES)):
                pass_on(piece).start()

        source = jnp.where(slot == NEAR, left, across)
        other_span = span[source]
        second = jnp.where(other_span < own_span, 0, 1)

        def give(piece):
            chunks = pl.ds(*PIECES[piece])
            return pltpu.make_async_remote_copy(
                src_ref=part.at[slot, chunks],
                dst_ref=back.at[slot, chunks],
                send_sem=part_send_sem,
                recv_sem=back_sem.at[slot],
                device_id={"ctx": source},
                device_id_type=MESH,
            )

        for piece, (first, count) in enumerate(PIECES):
            wait_all(got.at[slot, pl.ds(first, count)], recv_sem.at[slot, piece])
            chunks = range(first, first + count)
            block, before = divmod(first, CHUNKS // 2)
            if block == 0:
                at = 1
                blocks = [joined(*(got[slot, c, which] for c in chunks)) for which in range(2)]
            else:
                at = second
                blocks = [
                    joined(*(
                        jnp.where(second == 0, got[slot, c - CHUNKS // 2, which], got[slot, c, which]) for c in chunks
                    ))
                    for which in range(2)
                ]
            score_out = score_grads.at[PARTNER + 2 * slot + block, pl.ds(before * chunk, count * chunk)]
            terms = block_grads(*blocks, at, score_out)
            for which in range(2):
                for i, c in enumerate(chunks):
                    part[slot, c, which] = terms[which][i * chunk : (i + 1) * chunk].astype(BF16)
            give(piece).start()
        return 0

    lax.fori_loop(0, 2, partner, 0)

    near_early = span[left] < own_span
    far_early = span[across] < own_span

    def first_keys(slot):
        return block_of(got, 0, 0, (slot,))

    def second_keys(slot, early):
        return jnp.where(early, first_keys(slot), block_of(got, 1, 0, (slot,)))

    zero = jnp.zeros((half, width), BF16)
    near_second, far_second = second_keys(NEAR, near_early), second_keys(FAR, far_early)
    near_slot, far_slot = PARTNER + 2 * NEAR, PARTNER + 2 * FAR
    early_keys = joined(
        own_keys[0], jnp.where(near_early, near_second, zero), jnp.where(far_early, far_second, zero)
    ).T
    late_keys = joined(
        own_keys[0], own_keys[1], first_keys(NEAR), first_keys(FAR),
        jnp.where(near_early, zero, near_second), jnp.where(far_early, zero, far_second),
    ).T
    early_slots = (OWN_EE, near_slot + 1, far_slot + 1)
    late_slots = (OWN_LE, OWN_LL, near_slot, far_slot, near_slot + 1, far_slot + 1)
    stores = []
    for pair in range(heads // 2):
        cols = pl.ds(pair * 2 * half, 2 * half)
        for block, (key_side, slots) in enumerate(((early_keys, early_slots), (late_keys, late_slots))):
            scores = jnp.concatenate([score_grads[s, :, cols] for s in slots], axis=0)
            turned = (dot_nn(key_side, scores) * inv_root).astype(BF16)
            for i in range(2):
                query_out[pl.ds(block * half, half), pl.ds((2 * pair + i) * width, width)] = (
                    turned[:, i * half : (i + 1) * half].T
                )

    wait_all(got, send_sem)
    wait_all(part, part_send_sem)

    @pl.when(kind == 1)
    def _():
        wait_all(held, pass_sem)

    for slot in (FAR, NEAR):
        wait_all(back.at[slot], back_sem.at[slot])
    near_early_back = own_span < span[right]
    far_early_back = own_span < span[across]
    for which, (sums, out) in enumerate(((own_key, key_out), (own_value, value_out))):
        early, late = sums[0], sums[1]
        for slot, to_early in ((NEAR, near_early_back), (FAR, far_early_back)):
            term = block_of(back, 1, which, (slot,)).astype(F32)
            early = early + block_of(back, 0, which, (slot,)).astype(F32)
            early = early + jnp.where(to_early, term, 0.0)
            late = late + jnp.where(to_early, 0.0, term)
        out[pl.ds(0, half)] = early.astype(BF16)
        out[pl.ds(half, half)] = late.astype(BF16)


def place(query_grad, key_grad, value_grad, query_out, key_out, value_out, sem):
    copies = [
        pltpu.make_async_copy(source, target, sem.at[i])
        for i, (source, target) in enumerate(
            ((query_grad, query_out), (key_grad, key_out), (value_grad, value_out))
        )
    ]
    for copy in copies:
        copy.start()
    for copy in copies:
        copy.wait()


def local(query_rows, key_rows, value_rows, out_grad, log_norm, row_dot, span_order):
    n = lax.axis_size("ctx")
    rows, width = key_rows.shape
    heads, half = log_norm.shape[0], rows // 2
    hbm = pl.BlockSpec(memory_space=pltpu.HBM)
    vmem = pl.BlockSpec(memory_space=pltpu.VMEM)
    blocks = 8 * 3 * half * half * heads * 7
    key_pieces, value_pieces = (x.reshape(CHUNKS, rows // CHUNKS, width) for x in (key_rows, value_rows))
    args = (query_rows, key_pieces, value_pieces, out_grad, log_norm, row_dot, span_order)
    grads = pl.pallas_call(
        functools.partial(kernel, n, heads, half, width),
        name="attention_grads",
        out_shape=(
            pltpu.VMEM(query_rows.shape, BF16),
            pltpu.VMEM(key_rows.shape, BF16),
            pltpu.VMEM(value_rows.shape, BF16),
        ),
        in_specs=[hbm] * 7,
        out_specs=(vmem, vmem, vmem),
        scratch_shapes=[
            pltpu.VMEM((2, 2, half, heads * width), BF16),
            pltpu.VMEM((2, 2, heads, half), F32),
            pltpu.VMEM((CHUNKS, 2, rows // CHUNKS, width), BF16),
            pltpu.SMEM((n,), jnp.int32),
            pltpu.VMEM((2, CHUNKS, 2, rows // CHUNKS, width), BF16),
            pltpu.VMEM((CHUNKS, 2, rows // CHUNKS, width), BF16),
            pltpu.VMEM((2, CHUNKS, 2, rows // CHUNKS, width), BF16),
            pltpu.VMEM((2, CHUNKS, 2, rows // CHUNKS, width), BF16),
            pltpu.VMEM((7, half, heads * half), BF16),
            pltpu.VMEM((2, half, width), F32),
            pltpu.VMEM((2, half, width), F32),
            pltpu.SemaphoreType.REGULAR,
            pltpu.SemaphoreType.DMA((3,)),
            pltpu.SemaphoreType.DMA,
            pltpu.SemaphoreType.DMA,
            pltpu.SemaphoreType.DMA((2, len(PIECES))),
            pltpu.SemaphoreType.DMA,
            pltpu.SemaphoreType.DMA,
            pltpu.SemaphoreType.DMA,
            pltpu.SemaphoreType.DMA((2,)),
        ],
        compiler_params=pltpu.CompilerParams(
            collective_id=0, has_side_effects=True, vmem_limit_bytes=24 * 1024 * 1024
        ),
        cost_estimate=pl.CostEstimate(
            flops=10 * half * half * width * heads * 7, bytes_accessed=2 << 20, transcendentals=blocks // 24
        ),
    )(*[pltpu.with_memory_space_constraint(x, pltpu.HBM) for x in args])
    return pl.pallas_call(
        place,
        name="place_grads",
        out_shape=tuple(pltpu.HBM(g.shape, g.dtype) for g in grads),
        in_specs=[vmem] * 3,
        out_specs=(hbm,) * 3,
        scratch_shapes=[pltpu.SemaphoreType.DMA((3,))],
    )(*[pltpu.with_memory_space_constraint(g, pltpu.VMEM) for g in grads])


def solution(mesh):
    return jax.shard_map(
        local,
        mesh=mesh,
        in_specs=(
            P(("batch", "ctx"), None),
            P(("batch", "ctx"), None),
            P(("batch", "ctx"), None),
            P(("batch", "ctx"), None),
            P(None, ("batch", "ctx")),
            P(None, ("batch", "ctx")),
            P("batch"),
        ),
        out_specs=(P(("batch", "ctx"), None), P(("batch", "ctx"), None), P(("batch", "ctx"), None)),
        check_vma=False,
    )
```

```python
import functools
import math

import jax
import jax.numpy as jnp
from jax import lax
from jax.experimental import pallas as pl
from jax.experimental.pallas import tpu as pltpu
from jax.sharding import PartitionSpec as P

MESH = pl.DeviceIdType.MESH
BF16, F32 = jnp.bfloat16, jnp.float32
NEAR, FAR = 0, 1
OWN_EE, OWN_LE, OWN_LL, PARTNER = 0, 1, 2, 3
CHUNKS = 8
PIECES = ((0, 4), (4, 4))


def dot_nt(left, right):
    return lax.dot_general(left, right, (((1,), (1,)), ((), ())), preferred_element_type=F32)


def dot_nn(left, right):
    return jnp.dot(left, right, preferred_element_type=F32)


def kernel(
    n, heads, half, width,
    query_hbm, key_hbm, value_hbm, grad_hbm, norm_hbm, dot_hbm, span_hbm,
    query_out, key_out, value_out,
    sides, rows, own, span,
    got, held, part, back, score_grads, own_key, own_value,
    ready, load_sem, span_sem, send_sem, recv_sem, held_sem, pass_sem, part_send_sem, back_sem,
):
    me = lax.axis_index("ctx")
    right, left = lax.rem(me + 1, n), lax.rem(me + n - 1, n)
    across = lax.rem(me + n // 2, n)
    inv_root = 1.0 / math.sqrt(width)

    kind = lax.rem(me, 4)
    lane, lanes = lax.axis_index("batch"), lax.axis_size("batch")
    low = lane < lanes // 2
    via = jnp.where(low, lane + lanes // 2, lanes - 1 - lane)
    giver = jnp.where(low, lanes - 1 - lane, lane - lanes // 2)
    barrier = pltpu.get_barrier_semaphore()

    def tell(sem, device, at=lane):
        pl.semaphore_signal(sem, inc=1, device_id={"ctx": device, "batch": at}, device_id_type=MESH)

    @pl.when(kind == 2)
    def _():
        tell(barrier, right)
        tell(barrier, across)

    @pl.when(kind == 0)
    def _():
        tell(barrier, left)
        tell(barrier, across)

    @pl.when(kind == 1)
    def _():
        tell(barrier, lax.rem(me + 2, n), giver)
        tell(barrier, me, giver)
        tell(barrier, across)
        tell(barrier, left)

    @pl.when(kind == 3)
    def _():
        tell(barrier, left)

    chunk = 2 * half // CHUNKS
    query, grad, norm, dot = sides.at[0], sides.at[1], rows.at[0], rows.at[1]

    def load(source, target, group):
        pltpu.make_async_copy(source, target, load_sem.at[group]).start()

    def wait_all(ref, sem):
        pltpu.make_async_copy(ref, ref, sem).wait()

    for which, source in enumerate((key_hbm, value_hbm)):
        load(source, own.at[:, which], 0)

    def near_from_hbm():
        for piece, (first, count) in enumerate(PIECES):
            for which, source in enumerate((key_hbm, value_hbm)):
                pltpu.make_async_remote_copy(
                    src_ref=source.at[pl.ds(first, count)],
                    dst_ref=got.at[NEAR, pl.ds(first, count), which],
                    send_sem=send_sem,
                    recv_sem=recv_sem.at[NEAR, piece],
                    device_id={"ctx": right},
                    device_id_type=MESH,
                ).start()

    @pl.when(kind == 3)
    def _():
        pl.semaphore_wait(barrier, 3)
        tell(ready, lax.rem(me + n - 2, n), via)
        near_from_hbm()

    for which, source in enumerate((query_hbm, grad_hbm)):
        for block in range(2):
            load(source.at[pl.ds(block * half, half)], sides.at[which, block], 1)
    for which, source in enumerate((norm_hbm, dot_hbm)):
        for block in range(2):
            load(source.at[:, pl.ds(block * half, half)], rows.at[which, block], 2)
    span_load = pltpu.make_async_copy(span_hbm, span, span_sem)
    span_load.start()

    def offer(slot, piece, device):
        return pltpu.make_async_remote_copy(
            src_ref=own.at[pl.ds(*PIECES[piece])],
            dst_ref=got.at[slot, pl.ds(*PIECES[piece])],
            send_sem=send_sem,
            recv_sem=recv_sem.at[slot, piece],
            device_id={"ctx": device},
            device_id_type=MESH,
        )

    def hand():
        return pltpu.make_async_remote_copy(
            src_ref=own,
            dst_ref=held,
            send_sem=send_sem,
            recv_sem=held_sem,
            device_id={"ctx": me, "batch": via},
            device_id_type=MESH,
        )

    def pass_on(piece):
        return pltpu.make_async_remote_copy(
            src_ref=held.at[pl.ds(*PIECES[piece])],
            dst_ref=got.at[NEAR, pl.ds(*PIECES[piece])],
            send_sem=pass_sem,
            recv_sem=recv_sem.at[NEAR, piece],
            device_id={"ctx": right, "batch": giver},
            device_id_type=MESH,
        )

    def near_offers():
        for piece in range(len(PIECES)):
            offer(NEAR, piece, right).start()

    def far_offers():
        for piece in range(len(PIECES)):
            offer(FAR, piece, across).start()

    @pl.when(kind != 3)
    def _():
        pl.semaphore_wait(barrier, 2)

    wait_all(own, load_sem.at[0])

    @pl.when(kind == 1)
    def _():
        hand().start()

    @pl.when((kind == 0) | (kind == 2))
    def _():
        near_offers()

    @pl.when(kind == 3)
    def _():
        pl.semaphore_wait(ready, 1)

    far_offers()

    @pl.when(kind == 2)
    def _():
        tell(ready, across)
        pl.semaphore_wait(ready, 1)
        tell(ready, right)

    wait_all(sides, load_sem.at[1])
    wait_all(rows, load_sem.at[2])
    span_load.wait()
    own_span = span[me]

    causal = lax.broadcasted_iota(jnp.int32, (half, heads * half), 0) <= (
        lax.broadcasted_iota(jnp.int32, (half, heads * half), 1) % half
    )

    def by_head(ref, at):
        return jnp.concatenate([ref[at, :, pl.ds(h * width, width)] for h in range(heads)], axis=0)

    def by_row(ref, at):
        return jnp.concatenate([ref[at, pl.ds(h, 1), :] for h in range(heads)], axis=1)

    def block_grads(key_block, value_block, at, score_out, diagonal=False):
        query_all, grad_all = by_head(query, at), by_head(grad, at)
        weights = jnp.exp(dot_nt(key_block, query_all) * inv_root - by_row(norm, at))
        if diagonal:
            weights = jnp.where(causal, weights, 0.0)
        score_grad = (weights * (dot_nt(value_block, grad_all) - by_row(dot, at))).astype(BF16)
        score_out[...] = score_grad
        value_term = dot_nn(weights.astype(BF16), grad_all)
        return dot_nn(score_grad, query_all) * inv_root, value_term

    def joined(*pieces):
        return jnp.concatenate(pieces, axis=0)

    def block_of(ref, block, which, slot=()):
        chunks = range(block * CHUNKS // 2, (block + 1) * CHUNKS // 2)
        return joined(*(ref[(*slot, c, which)] for c in chunks))

    own_keys = [block_of(own, block, 0) for block in range(2)]
    own_values = [block_of(own, block, 1) for block in range(2)]
    key_term, value_term = block_grads(own_keys[0], own_values[0], 0, score_grads.at[OWN_EE], True)
    key_more, value_more = block_grads(own_keys[0], own_values[0], 1, score_grads.at[OWN_LE])
    own_key[0] = key_term + key_more
    own_value[0] = value_term + value_more
    own_key[1], own_value[1] = block_grads(own_keys[1], own_values[1], 1, score_grads.at[OWN_LL], True)

    far_first = jnp.where(kind == 0, 1, 0)

    def partner(step, _):
        slot = lax.rem(step + far_first, 2)

        @pl.when((kind == 1) & (step == 1))
        def _():
            pl.semaphore_wait(ready, 1)
            hand().wait_recv()
            for piece in range(len(PIECES)):
                pass_on(piece).start()

        source = jnp.where(slot == NEAR, left, across)
        other_span = span[source]
        second = jnp.where(other_span < own_span, 0, 1)

        def give(piece):
            chunks = pl.ds(*PIECES[piece])
            return pltpu.make_async_remote_copy(
                src_ref=part.at[slot, chunks],
                dst_ref=back.at[slot, chunks],
                send_sem=part_send_sem,
                recv_sem=back_sem.at[slot],
                device_id={"ctx": source},
                device_id_type=MESH,
            )

        for piece, (first, count) in enumerate(PIECES):
            wait_all(got.at[slot, pl.ds(first, count)], recv_sem.at[slot, piece])
            chunks = range(first, first + count)
            block, before = divmod(first, CHUNKS // 2)
            if block == 0:
                at = 1
                blocks = [joined(*(got[slot, c, which] for c in chunks)) for which in range(2)]
            else:
                at = second
                blocks = [
                    joined(*(
                        jnp.where(second == 0, got[slot, c - CHUNKS // 2, which], got[slot, c, which]) for c in chunks
                    ))
                    for which in range(2)
                ]
            score_out = score_grads.at[PARTNER + 2 * slot + block, pl.ds(before * chunk, count * chunk)]
            terms = block_grads(*blocks, at, score_out)
            for which in range(2):
                for i, c in enumerate(chunks):
                    part[slot, c, which] = terms[which][i * chunk : (i + 1) * chunk].astype(BF16)
            give(piece).start()
        return 0

    lax.fori_loop(0, 2, partner, 0)

    near_early = span[left] < own_span
    far_early = span[across] < own_span

    def first_keys(slot):
        return block_of(got, 0, 0, (slot,))

    def second_keys(slot, early):
        return jnp.where(early, first_keys(slot), block_of(got, 1, 0, (slot,)))

    zero = jnp.zeros((half, width), BF16)
    near_second, far_second = second_keys(NEAR, near_early), second_keys(FAR, far_early)
    near_slot, far_slot = PARTNER + 2 * NEAR, PARTNER + 2 * FAR
    early_keys = joined(
        own_keys[0], jnp.where(near_early, near_second, zero), jnp.where(far_early, far_second, zero)
    ).T
    late_keys = joined(
        own_keys[0], own_keys[1], first_keys(NEAR), first_keys(FAR),
        jnp.where(near_early, zero, near_second), jnp.where(far_early, zero, far_second),
    ).T
    early_slots = (OWN_EE, near_slot + 1, far_slot + 1)
    late_slots = (OWN_LE, OWN_LL, near_slot, far_slot, near_slot + 1, far_slot + 1)
    stores = []
    for pair in range(heads // 2):
        cols = pl.ds(pair * 2 * half, 2 * half)
        for block, (key_side, slots) in enumerate(((early_keys, early_slots), (late_keys, late_slots))):
            scores = jnp.concatenate([score_grads[s, :, cols] for s in slots], axis=0)
            turned = (dot_nn(key_side, scores) * inv_root).astype(BF16)
            for i in range(2):
                query_out[pl.ds(block * half, half), pl.ds((2 * pair + i) * width, width)] = (
                    turned[:, i * half : (i + 1) * half].T
                )

    wait_all(got, send_sem)
    wait_all(part, part_send_sem)

    @pl.when(kind == 1)
    def _():
        wait_all(held, pass_sem)

    def add_returned(slot, early_back, which, early, late):
        term = block_of(back, 1, which, (slot,)).astype(F32)
        early = early + block_of(back, 0, which, (slot,)).astype(F32)
        return early + jnp.where(early_back, term, 0.0), late + jnp.where(early_back, 0.0, term)

    wait_all(back.at[FAR], back_sem.at[FAR])
    for which, sums in enumerate((own_key, own_value)):
        sums[0], sums[1] = add_returned(FAR, own_span < span[across], which, sums[0], sums[1])
    wait_all(back.at[NEAR], back_sem.at[NEAR])
    for which, (sums, out) in enumerate(((own_key, key_out), (own_value, value_out))):
        early, late = add_returned(NEAR, own_span < span[right], which, sums[0], sums[1])
        out[pl.ds(0, half)] = early.astype(BF16)
        out[pl.ds(half, half)] = late.astype(BF16)


def place(query_grad, key_grad, value_grad, query_out, key_out, value_out, sem):
    copies = [
        pltpu.make_async_copy(source, target, sem.at[i])
        for i, (source, target) in enumerate(
            ((query_grad, query_out), (key_grad, key_out), (value_grad, value_out))
        )
    ]
    for copy in copies:
        copy.start()
    for copy in copies:
        copy.wait()


def local(query_rows, key_rows, value_rows, out_grad, log_norm, row_dot, span_order):
    n = lax.axis_size("ctx")
    rows, width = key_rows.shape
    heads, half = log_norm.shape[0], rows // 2
    hbm = pl.BlockSpec(memory_space=pltpu.HBM)
    vmem = pl.BlockSpec(memory_space=pltpu.VMEM)
    blocks = 8 * 3 * half * half * heads * 7
    key_pieces, value_pieces = (x.reshape(CHUNKS, rows // CHUNKS, width) for x in (key_rows, value_rows))
    args = (query_rows, key_pieces, value_pieces, out_grad, log_norm, row_dot, span_order)
    grads = pl.pallas_call(
        functools.partial(kernel, n, heads, half, width),
        name="attention_grads",
        out_shape=(
            pltpu.VMEM(query_rows.shape, BF16),
            pltpu.VMEM(key_rows.shape, BF16),
            pltpu.VMEM(value_rows.shape, BF16),
        ),
        in_specs=[hbm] * 7,
        out_specs=(vmem, vmem, vmem),
        scratch_shapes=[
            pltpu.VMEM((2, 2, half, heads * width), BF16),
            pltpu.VMEM((2, 2, heads, half), F32),
            pltpu.VMEM((CHUNKS, 2, rows // CHUNKS, width), BF16),
            pltpu.SMEM((n,), jnp.int32),
            pltpu.VMEM((2, CHUNKS, 2, rows // CHUNKS, width), BF16),
            pltpu.VMEM((CHUNKS, 2, rows // CHUNKS, width), BF16),
            pltpu.VMEM((2, CHUNKS, 2, rows // CHUNKS, width), BF16),
            pltpu.VMEM((2, CHUNKS, 2, rows // CHUNKS, width), BF16),
            pltpu.VMEM((7, half, heads * half), BF16),
            pltpu.VMEM((2, half, width), F32),
            pltpu.VMEM((2, half, width), F32),
            pltpu.SemaphoreType.REGULAR,
            pltpu.SemaphoreType.DMA((3,)),
            pltpu.SemaphoreType.DMA,
            pltpu.SemaphoreType.DMA,
            pltpu.SemaphoreType.DMA((2, len(PIECES))),
            pltpu.SemaphoreType.DMA,
            pltpu.SemaphoreType.DMA,
            pltpu.SemaphoreType.DMA,
            pltpu.SemaphoreType.DMA((2,)),
        ],
        compiler_params=pltpu.CompilerParams(
            collective_id=0, has_side_effects=True, vmem_limit_bytes=24 * 1024 * 1024
        ),
        cost_estimate=pl.CostEstimate(
            flops=10 * half * half * width * heads * 7, bytes_accessed=2 << 20, transcendentals=blocks // 24
        ),
    )(*[pltpu.with_memory_space_constraint(x, pltpu.HBM) for x in args])
    return pl.pallas_call(
        place,
        name="place_grads",
        out_shape=tuple(pltpu.HBM(g.shape, g.dtype) for g in grads),
        in_specs=[vmem] * 3,
        out_specs=(hbm,) * 3,
        scratch_shapes=[pltpu.SemaphoreType.DMA((3,))],
    )(*[pltpu.with_memory_space_constraint(g, pltpu.VMEM) for g in grads])


def solution(mesh):
    return jax.shard_map(
        local,
        mesh=mesh,
        in_specs=(
            P(("batch", "ctx"), None),
            P(("batch", "ctx"), None),
            P(("batch", "ctx"), None),
            P(("batch", "ctx"), None),
            P(None, ("batch", "ctx")),
            P(None, ("batch", "ctx")),
            P("batch"),
        ),
        out_specs=(P(("batch", "ctx"), None), P(("batch", "ctx"), None), P(("batch", "ctx"), None)),
        check_vma=False,
    )
```

```python
import functools
import math

import jax
import jax.numpy as jnp
from jax import lax
from jax.experimental import pallas as pl
from jax.experimental.pallas import tpu as pltpu
from jax.sharding import PartitionSpec as P

MESH = pl.DeviceIdType.MESH
BF16, F32 = jnp.bfloat16, jnp.float32
NEAR, FAR = 0, 1
OWN_EE, OWN_LE, OWN_LL, PARTNER = 0, 1, 2, 3
CHUNKS = 8
PIECES = ((0, 4), (4, 4))


def dot_nt(left, right):
    return lax.dot_general(left, right, (((1,), (1,)), ((), ())), preferred_element_type=F32)


def dot_nn(left, right):
    return jnp.dot(left, right, preferred_element_type=F32)


def kernel(
    n, heads, half, width,
    query_hbm, key_hbm, value_hbm, grad_hbm, norm_hbm, dot_hbm, span_hbm,
    query_out, key_out, value_out,
    sides, rows, own, span,
    got, held, part, back, score_grads, own_key, own_value,
    ready, load_sem, span_sem, send_sem, recv_sem, held_sem, pass_sem, part_send_sem, back_sem,
):
    me = lax.axis_index("ctx")
    right, left = lax.rem(me + 1, n), lax.rem(me + n - 1, n)
    across = lax.rem(me + n // 2, n)
    inv_root = 1.0 / math.sqrt(width)

    kind = lax.rem(me, 4)
    lane, lanes = lax.axis_index("batch"), lax.axis_size("batch")
    low = lane < lanes // 2
    via = jnp.where(low, lane + lanes // 2, lanes - 1 - lane)
    giver = jnp.where(low, lanes - 1 - lane, lane - lanes // 2)
    barrier = pltpu.get_barrier_semaphore()

    def tell(sem, device, at=lane):
        pl.semaphore_signal(sem, inc=1, device_id={"ctx": device, "batch": at}, device_id_type=MESH)

    @pl.when(kind == 2)
    def _():
        tell(barrier, right)
        tell(barrier, across)

    @pl.when(kind == 0)
    def _():
        tell(barrier, left)
        tell(barrier, across)

    @pl.when(kind == 1)
    def _():
        tell(barrier, lax.rem(me + 2, n), giver)
        tell(barrier, me, giver)
        tell(barrier, across)
        tell(barrier, left)

    @pl.when(kind == 3)
    def _():
        tell(barrier, left)

    chunk = 2 * half // CHUNKS
    query, grad, norm, dot = sides.at[0], sides.at[1], rows.at[0], rows.at[1]

    def load(source, target, group):
        pltpu.make_async_copy(source, target, load_sem.at[group]).start()

    def wait_all(ref, sem):
        pltpu.make_async_copy(ref, ref, sem).wait()

    def near_from_hbm():
        for piece, (first, count) in enumerate(PIECES):
            for which, source in enumerate((key_hbm, value_hbm)):
                pltpu.make_async_remote_copy(
                    src_ref=source.at[pl.ds(first, count)],
                    dst_ref=got.at[NEAR, pl.ds(first, count), which],
                    send_sem=send_sem,
                    recv_sem=recv_sem.at[NEAR, piece],
                    device_id={"ctx": right},
                    device_id_type=MESH,
                ).start()

    @pl.when(kind == 3)
    def _():
        pl.semaphore_wait(barrier, 3)
        tell(ready, lax.rem(me + n - 2, n), via)
        near_from_hbm()

    for which, source in enumerate((key_hbm, value_hbm)):
        load(source, own.at[:, which], 0)

    for which, source in enumerate((query_hbm, grad_hbm)):
        for block in range(2):
            load(source.at[pl.ds(block * half, half)], sides.at[which, block], 1)
    for which, source in enumerate((norm_hbm, dot_hbm)):
        for block in range(2):
            load(source.at[:, pl.ds(block * half, half)], rows.at[which, block], 2)
    span_load = pltpu.make_async_copy(span_hbm, span, span_sem)
    span_load.start()

    def offer(slot, piece, device):
        return pltpu.make_async_remote_copy(
            src_ref=own.at[pl.ds(*PIECES[piece])],
            dst_ref=got.at[slot, pl.ds(*PIECES[piece])],
            send_sem=send_sem,
            recv_sem=recv_sem.at[slot, piece],
            device_id={"ctx": device},
            device_id_type=MESH,
        )

    def hand():
        return pltpu.make_async_remote_copy(
            src_ref=own,
            dst_ref=held,
            send_sem=send_sem,
            recv_sem=held_sem,
            device_id={"ctx": me, "batch": via},
            device_id_type=MESH,
        )

    def pass_on(piece):
        return pltpu.make_async_remote_copy(
            src_ref=held.at[pl.ds(*PIECES[piece])],
            dst_ref=got.at[NEAR, pl.ds(*PIECES[piece])],
            send_sem=pass_sem,
            recv_sem=recv_sem.at[NEAR, piece],
            device_id={"ctx": right, "batch": giver},
            device_id_type=MESH,
        )

    def near_offers():
        for piece in range(len(PIECES)):
            offer(NEAR, piece, right).start()

    def far_offers():
        for piece in range(len(PIECES)):
            offer(FAR, piece, across).start()

    @pl.when(kind != 3)
    def _():
        pl.semaphore_wait(barrier, 2)

    wait_all(own, load_sem.at[0])

    @pl.when(kind == 1)
    def _():
        hand().start()

    @pl.when((kind == 0) | (kind == 2))
    def _():
        near_offers()

    @pl.when(kind == 3)
    def _():
        pl.semaphore_wait(ready, 1)

    far_offers()

    @pl.when(kind == 2)
    def _():
        tell(ready, across)
        pl.semaphore_wait(ready, 1)
        tell(ready, right)

    wait_all(sides, load_sem.at[1])
    wait_all(rows, load_sem.at[2])
    span_load.wait()
    own_span = span[me]

    causal = lax.broadcasted_iota(jnp.int32, (half, heads * half), 0) <= (
        lax.broadcasted_iota(jnp.int32, (half, heads * half), 1) % half
    )

    def by_head(ref, at):
        return jnp.concatenate([ref[at, :, pl.ds(h * width, width)] for h in range(heads)], axis=0)

    def by_row(ref, at):
        return jnp.concatenate([ref[at, pl.ds(h, 1), :] for h in range(heads)], axis=1)

    def block_grads(key_block, value_block, at, score_out, diagonal=False):
        query_all, grad_all = by_head(query, at), by_head(grad, at)
        weights = jnp.exp(dot_nt(key_block, query_all) * inv_root - by_row(norm, at))
        if diagonal:
            weights = jnp.where(causal, weights, 0.0)
        score_grad = (weights * (dot_nt(value_block, grad_all) - by_row(dot, at))).astype(BF16)
        score_out[...] = score_grad
        value_term = dot_nn(weights.astype(BF16), grad_all)
        return dot_nn(score_grad, query_all) * inv_root, value_term

    def joined(*pieces):
        return jnp.concatenate(pieces, axis=0)

    def block_of(ref, block, which, slot=()):
        chunks = range(block * CHUNKS // 2, (block + 1) * CHUNKS // 2)
        return joined(*(ref[(*slot, c, which)] for c in chunks))

    own_keys = [block_of(own, block, 0) for block in range(2)]
    own_values = [block_of(own, block, 1) for block in range(2)]
    key_term, value_term = block_grads(own_keys[0], own_values[0], 0, score_grads.at[OWN_EE], True)
    key_more, value_more = block_grads(own_keys[0], own_values[0], 1, score_grads.at[OWN_LE])
    own_key[0] = key_term + key_more
    own_value[0] = value_term + value_more
    own_key[1], own_value[1] = block_grads(own_keys[1], own_values[1], 1, score_grads.at[OWN_LL], True)

    far_first = jnp.where(kind == 0, 1, 0)

    def partner(step, _):
        slot = lax.rem(step + far_first, 2)

        @pl.when((kind == 1) & (step == 1))
        def _():
            pl.semaphore_wait(ready, 1)
            hand().wait_recv()
            for piece in range(len(PIECES)):
                pass_on(piece).start()

        source = jnp.where(slot == NEAR, left, across)
        other_span = span[source]
        second = jnp.where(other_span < own_span, 0, 1)

        def give(piece):
            chunks = pl.ds(*PIECES[piece])
            return pltpu.make_async_remote_copy(
                src_ref=part.at[slot, chunks],
                dst_ref=back.at[slot, chunks],
                send_sem=part_send_sem,
                recv_sem=back_sem.at[slot],
                device_id={"ctx": source},
                device_id_type=MESH,
            )

        for piece, (first, count) in enumerate(PIECES):
            wait_all(got.at[slot, pl.ds(first, count)], recv_sem.at[slot, piece])
            chunks = range(first, first + count)
            block, before = divmod(first, CHUNKS // 2)
            if block == 0:
                at = 1
                blocks = [joined(*(got[slot, c, which] for c in chunks)) for which in range(2)]
            else:
                at = second
                blocks = [
                    joined(*(
                        jnp.where(second == 0, got[slot, c - CHUNKS // 2, which], got[slot, c, which]) for c in chunks
                    ))
                    for which in range(2)
                ]
            score_out = score_grads.at[PARTNER + 2 * slot + block, pl.ds(before * chunk, count * chunk)]
            terms = block_grads(*blocks, at, score_out)
            for which in range(2):
                for i, c in enumerate(chunks):
                    part[slot, c, which] = terms[which][i * chunk : (i + 1) * chunk].astype(BF16)
            give(piece).start()
        return 0

    lax.fori_loop(0, 2, partner, 0)

    near_early = span[left] < own_span
    far_early = span[across] < own_span

    def first_keys(slot):
        return block_of(got, 0, 0, (slot,))

    def second_keys(slot, early):
        return jnp.where(early, first_keys(slot), block_of(got, 1, 0, (slot,)))

    zero = jnp.zeros((half, width), BF16)
    near_second, far_second = second_keys(NEAR, near_early), second_keys(FAR, far_early)
    near_slot, far_slot = PARTNER + 2 * NEAR, PARTNER + 2 * FAR
    early_keys = joined(
        own_keys[0], jnp.where(near_early, near_second, zero), jnp.where(far_early, far_second, zero)
    ).T
    late_keys = joined(
        own_keys[0], own_keys[1], first_keys(NEAR), first_keys(FAR),
        jnp.where(near_early, zero, near_second), jnp.where(far_early, zero, far_second),
    ).T
    early_slots = (OWN_EE, near_slot + 1, far_slot + 1)
    late_slots = (OWN_LE, OWN_LL, near_slot, far_slot, near_slot + 1, far_slot + 1)
    stores = []
    for pair in range(heads // 2):
        cols = pl.ds(pair * 2 * half, 2 * half)
        for block, (key_side, slots) in enumerate(((early_keys, early_slots), (late_keys, late_slots))):
            scores = jnp.concatenate([score_grads[s, :, cols] for s in slots], axis=0)
            turned = (dot_nn(key_side, scores) * inv_root).astype(BF16)
            for i in range(2):
                query_out[pl.ds(block * half, half), pl.ds((2 * pair + i) * width, width)] = (
                    turned[:, i * half : (i + 1) * half].T
                )

    wait_all(got, send_sem)
    wait_all(part, part_send_sem)

    @pl.when(kind == 1)
    def _():
        wait_all(held, pass_sem)

    def add_returned(slot, early_back, which, early, late):
        term = block_of(back, 1, which, (slot,)).astype(F32)
        early = early + block_of(back, 0, which, (slot,)).astype(F32)
        return early + jnp.where(early_back, term, 0.0), late + jnp.where(early_back, 0.0, term)

    wait_all(back.at[FAR], back_sem.at[FAR])
    for which, sums in enumerate((own_key, own_value)):
        sums[0], sums[1] = add_returned(FAR, own_span < span[across], which, sums[0], sums[1])
    wait_all(back.at[NEAR], back_sem.at[NEAR])
    for which, (sums, out) in enumerate(((own_key, key_out), (own_value, value_out))):
        early, late = add_returned(NEAR, own_span < span[right], which, sums[0], sums[1])
        out[pl.ds(0, half)] = early.astype(BF16)
        out[pl.ds(half, half)] = late.astype(BF16)


def place(query_grad, key_grad, value_grad, query_out, key_out, value_out, sem):
    copies = [
        pltpu.make_async_copy(source, target, sem.at[i])
        for i, (source, target) in enumerate(
            ((query_grad, query_out), (key_grad, key_out), (value_grad, value_out))
        )
    ]
    for copy in copies:
        copy.start()
    for copy in copies:
        copy.wait()


def local(query_rows, key_rows, value_rows, out_grad, log_norm, row_dot, span_order):
    n = lax.axis_size("ctx")
    rows, width = key_rows.shape
    heads, half = log_norm.shape[0], rows // 2
    hbm = pl.BlockSpec(memory_space=pltpu.HBM)
    vmem = pl.BlockSpec(memory_space=pltpu.VMEM)
    blocks = 8 * 3 * half * half * heads * 7
    key_pieces, value_pieces = (x.reshape(CHUNKS, rows // CHUNKS, width) for x in (key_rows, value_rows))
    args = (query_rows, key_pieces, value_pieces, out_grad, log_norm, row_dot, span_order)
    grads = pl.pallas_call(
        functools.partial(kernel, n, heads, half, width),
        name="attention_grads",
        out_shape=(
            pltpu.VMEM(query_rows.shape, BF16),
            pltpu.VMEM(key_rows.shape, BF16),
            pltpu.VMEM(value_rows.shape, BF16),
        ),
        in_specs=[hbm] * 7,
        out_specs=(vmem, vmem, vmem),
        scratch_shapes=[
            pltpu.VMEM((2, 2, half, heads * width), BF16),
            pltpu.VMEM((2, 2, heads, half), F32),
            pltpu.VMEM((CHUNKS, 2, rows // CHUNKS, width), BF16),
            pltpu.SMEM((n,), jnp.int32),
            pltpu.VMEM((2, CHUNKS, 2, rows // CHUNKS, width), BF16),
            pltpu.VMEM((CHUNKS, 2, rows // CHUNKS, width), BF16),
            pltpu.VMEM((2, CHUNKS, 2, rows // CHUNKS, width), BF16),
            pltpu.VMEM((2, CHUNKS, 2, rows // CHUNKS, width), BF16),
            pltpu.VMEM((7, half, heads * half), BF16),
            pltpu.VMEM((2, half, width), F32),
            pltpu.VMEM((2, half, width), F32),
            pltpu.SemaphoreType.REGULAR,
            pltpu.SemaphoreType.DMA((3,)),
            pltpu.SemaphoreType.DMA,
            pltpu.SemaphoreType.DMA,
            pltpu.SemaphoreType.DMA((2, len(PIECES))),
            pltpu.SemaphoreType.DMA,
            pltpu.SemaphoreType.DMA,
            pltpu.SemaphoreType.DMA,
            pltpu.SemaphoreType.DMA((2,)),
        ],
        compiler_params=pltpu.CompilerParams(
            collective_id=0, has_side_effects=True, vmem_limit_bytes=24 * 1024 * 1024
        ),
        cost_estimate=pl.CostEstimate(
            flops=10 * half * half * width * heads * 7, bytes_accessed=2 << 20, transcendentals=blocks // 24
        ),
    )(*[pltpu.with_memory_space_constraint(x, pltpu.HBM) for x in args])
    return pl.pallas_call(
        place,
        name="place_grads",
        out_shape=tuple(pltpu.HBM(g.shape, g.dtype) for g in grads),
        in_specs=[vmem] * 3,
        out_specs=(hbm,) * 3,
        scratch_shapes=[pltpu.SemaphoreType.DMA((3,))],
    )(*[pltpu.with_memory_space_constraint(g, pltpu.VMEM) for g in grads])


def solution(mesh):
    return jax.shard_map(
        local,
        mesh=mesh,
        in_specs=(
            P(("batch", "ctx"), None),
            P(("batch", "ctx"), None),
            P(("batch", "ctx"), None),
            P(("batch", "ctx"), None),
            P(None, ("batch", "ctx")),
            P(None, ("batch", "ctx")),
            P("batch"),
        ),
        out_specs=(P(("batch", "ctx"), None), P(("batch", "ctx"), None), P(("batch", "ctx"), None)),
        check_vma=False,
    )
```
